512 devices in a mesh: rows: 64 (over z, x, core), heads: 8 (over y).
Axes of the slice: x: 4, y: 8, z: 8, core: 2. Of those that a mesh axis runs over, the one named last changes fastest.
Arguments:
- queries: bfloat16 [1024, 6144], P('rows', 'heads'), may hold values from -8 to 8
- keys: bfloat16 [65536, 6144], P('rows', 'heads'), may hold values from -8 to 8
- values: bfloat16 [65536, 6144], P('rows', 'heads'), may hold values from -6 to 6
- pattern: int32 [8, 16], replicated, may hold values from 0 to 63, all different within a row; in each aligned block of 8 rows (0 to 7, 8 to 15, ...) at most 4 rows name the same one
- out_weight: bfloat16 [6144, 6144], P('heads', 'rows'), may hold values from -0.5 to 0.5
Outputs:
- projected: bfloat16 [1024, 6144], P('heads', 'rows')
The draws below stay inside these ranges and needn't reach their ends.
Inputs may be any that keep to these rules, and one draw needn't show every extreme that they name: `pattern`: each row names 16 different cache blocks; no cache block is named by more than 4 rows, one by exactly 4; every cache block is named by some row.
All inputs are finite; a program needn't handle non-finite values.
Results may differ from the reference program's by a relative error of at most 0.0051.
Values may be sent and summed in bfloat16 or wider, within the bound.
A program may use at most 64 MiB of HBM per device.

```python
import math
import jax
import jax.numpy as jnp
import numpy as np
from jax import lax

D = 6144
HD = 128
QB = 128
CBLK = 1024
LINKS = 16
H = 48
QTOK = 1024
NQB = 8
CROWS = 65536
MOST = 4
N_ROWS = 64


def draw_queries(key, part):
    key = jax.random.fold_in(key, 1)
    base_key = jax.random.fold_in(key, 0)
    result = jnp.clip(1.5 * jax.random.normal(base_key, (QTOK, H * HD)), -8.0, 8.0)
    return result.astype(jnp.bfloat16)


def draw_keys(key, part):
    key = jax.random.fold_in(key, 2)
    result = jnp.clip(1.5 * jax.random.normal(key, (CROWS, H * HD)), -8.0, 8.0)
    return result.astype(jnp.bfloat16)


def steps_of(rng, extent, shards, smallest, top_value):
    factor_of = 1.0
    for dim, shards_of in shards:
        steps = jax.random.uniform(jax.random.fold_in(jax.random.fold_in(rng, 6), dim), (shards_of,), jnp.float32, smallest / len(shards), top_value / len(shards))
        factor_of = factor_of * jnp.repeat(jnp.exp(steps), extent[dim] // shards_of).reshape((-1,) + (1,) * (len(extent) - 1 - dim))
    return factor_of


def shared_out(stream_key, own, number, rows, amount, top, bound, lean):
    ranking = jax.random.permutation(stream_key, amount)
    packed, common = portions_of(amount, rows * top, bound, lean, True), portions_of(amount, rows * top, bound, lean, False)
    places = jnp.arange(amount)

    def named(sizes, offset_by):
        used = int((sizes > 0).sum())
        fixed = max(1, used // 4)
        shifted = fixed + (places - fixed + offset_by * (used - fixed)) % max(1, amount - fixed)
        return jnp.zeros((amount,), jnp.int32).at[ranking[jnp.where(places < fixed, places, shifted)]].set(jnp.asarray(sizes, jnp.int32))

    sizes = jnp.where(number % 4 == 0, named(packed, number // 4), named(common, number - number // 4 - 1))
    mixed = jax.random.permutation(jax.random.fold_in(own, 3), amount)
    giver, sink = mixed[0:amount // 2 * 2:2], mixed[1:amount // 2 * 2:2]
    room = jnp.minimum(sizes[giver] - 1, bound - sizes[sink]) // 2
    room = jnp.where((giver == ranking[0]) | (sink == ranking[0]) | (sizes[sink] == 0), 0, jnp.maximum(room, 0))
    shifted = jax.random.randint(jax.random.fold_in(own, 4), (amount // 2,), 0, 1 << 20) % (room + 1)
    sizes = sizes.at[giver].add(-shifted).at[sink].add(shifted)
    items = jnp.searchsorted(jnp.cumsum(sizes), jnp.arange(rows * top), side="right").astype(jnp.int32)
    listing = items.reshape(top, rows).T
    listing = listing[jax.random.permutation(jax.random.fold_in(own, 1), rows)]
    offset_by = jax.random.randint(jax.random.fold_in(own, 2), (rows, 1), 0, top)
    return jnp.take_along_axis(listing, (jnp.arange(top)[None, :] + offset_by) % top, axis=1)


def portions_of(amount, total, bound, slope, full):
    weights = [(1 << 20) // math.isqrt(grade ** slope) + 1 for grade in range(1, amount + 1)]
    largest = bound if full else min(bound, max(-(-total // amount), total * weights[0] // sum(weights)))
    least = 1 if total - largest >= amount - 1 else 0
    holding, surplus = [largest] + [least] * (amount - 1), total - largest - least * (amount - 1)
    while surplus > 0:
        candidates = [i for i in range(1, amount) if holding[i] < largest] or [i for i in range(1, amount) if holding[i] < bound]
        whole, left = sum([weights[i] for i in candidates]), surplus
        for i in candidates:
            addition = min(bound - holding[i], max(1, left * weights[i] // whole), surplus)
            holding[i] = holding[i] + addition
            surplus = surplus - addition
    return np.array(holding)


def centred(own_key, shape, scale, limit, cuts=(), kind=jnp.bfloat16):
    values = scale * jax.random.normal(own_key, shape, jnp.float32)
    if cuts:
        values = values * steps_of(own_key, shape, cuts, -0.22, 0.18)
    return jnp.clip(values, -limit, limit).astype(kind)


def setup_inputs(seed: int = 0) -> dict:
    arg_keys = jax.random.split(jax.random.key(seed), 6)
    queries = draw_queries(jax.random.fold_in(arg_keys[5], 71), 0)
    keys = draw_keys(jax.random.fold_in(arg_keys[5], 71), 0)
    values = centred(arg_keys[2], (CROWS, H * HD), 1.0, 6.0, ((0, 64), (1, 8)))
    pattern_keys = jax.random.split(jax.random.fold_in(arg_keys[3], 1), NQB // NQB)
    pattern_turns = jax.random.permutation(jax.random.fold_in(arg_keys[3], 3), NQB // NQB)
    pattern = jax.vmap(lambda own, number: shared_out(jax.random.fold_in(arg_keys[3], 2), own, number, NQB, N_ROWS, LINKS, MOST, 1))(pattern_keys, pattern_turns).reshape((NQB, LINKS))
    out_weight = centred(arg_keys[4], (H * HD, D), HD ** -0.5, 0.5, ((0, 8), (1, 64)))
    return {"queries": queries, "keys": keys, "values": values, "pattern": pattern, "out_weight": out_weight}


def block_partial(query_block, key_heads, value_heads):
    scores = jnp.einsum("qhd,khd->hqk", query_block.astype(jnp.float32), key_heads.astype(jnp.float32)) * (HD ** -0.5)
    row_max = jnp.max(scores, axis=2)
    exp_scores = jnp.exp(scores - row_max[:, :, None])
    row_total = jnp.sum(exp_scores, axis=2)
    weights = exp_scores.astype(jnp.bfloat16)
    mixed_out = jnp.einsum("hqk,khd->qhd", weights.astype(jnp.float32), value_heads.astype(jnp.float32))
    normed = mixed_out / row_total.T[:, :, None]
    return normed, (row_max + jnp.log(row_total)).T


def reference(queries, keys, values, pattern, out_weight):
    query_blocks = queries.reshape(NQB, QB, H, HD)
    key_blocks = keys.reshape(N_ROWS, CBLK, H, HD)
    value_blocks = values.reshape(N_ROWS, CBLK, H, HD)

    def one_query(pair_in):
        query_block, link_ids = pair_in

        def one_link(block_id):
            key_heads = lax.dynamic_index_in_dim(key_blocks, block_id, 0, keepdims=False)
            value_heads = lax.dynamic_index_in_dim(value_blocks, block_id, 0, keepdims=False)
            return block_partial(query_block, key_heads, value_heads)

        partials, lses = lax.map(one_link, link_ids)
        row_max = jnp.max(lses, axis=0)
        factor = jnp.exp(lses - row_max[None])
        numerator = jnp.sum(factor[..., None] * partials, axis=0)
        denominator = jnp.sum(factor, axis=0)
        return (numerator / denominator[..., None]).reshape(QB, H * HD).astype(jnp.bfloat16)

    attended = lax.map(one_query, (query_blocks, pattern)).reshape(QTOK, H * HD)
    return jnp.dot(attended, out_weight, preferred_element_type=jnp.float32).astype(jnp.bfloat16)
```

```python
import functools
import math

import jax
import jax.numpy as jnp
from jax import lax
from jax.experimental import pallas as pl
from jax.experimental.pallas import tpu as pltpu
from jax.sharding import PartitionSpec as P

MESH = pl.DeviceIdType.MESH
HD = 128
QB = 128
MOST = 4
CORES = 2
XN = 4
STATS = 16
LOW = -(2.0**100)
NT = (((1,), (1,)), ((), ()))
BF = jnp.bfloat16
F32 = jnp.float32


def near_first(n):
    order = []
    for step in range(1, n // 2 + 1):
        order.append(step)
        if n - step != step:
            order.append(n - step)
    return order


def kernel(
    q_ref,
    k_ref,
    v_ref,
    pat_ref,
    w_ref,
    out_ref,
    q_all,
    k_buf,
    v_buf,
    v_t,
    w_in,
    w_t,
    w_all,
    q_sel,
    num,
    top,
    tot,
    parts,
    parts_in,
    sums,
    sums_in,
    att,
    acc,
    acc_in,
    masks,
    local_sem,
    qz_s,
    qz_r,
    qx_s,
    qx_r,
    kv_s,
    kv_r,
    w_s,
    w_r,
    rx_s,
    rx_r,
    rz_s,
    rz_r,
    az_s,
    az_r,
    ax_s,
    ax_r,
    sib_s,
    sib_r,
    ready,
):
    r = lax.axis_index("rows")
    y = lax.axis_index("heads")
    yn = w_all.shape[0]
    zn = att.shape[0]
    nb = zn
    heads = num.shape[2] // HD
    half = heads * HD
    dq = HD // XN
    body = heads * dq
    own = q_ref.shape[0]
    z = r // (XN * CORES)
    x = (r // CORES) % XN
    c = r % CORES
    sib = 1 - c

    def dev(dz, dx, dc, dy):
        return ((dz * XN + dx) * CORES + dc, dy)

    def remote(src, dst, ss, rs, to):
        return pltpu.make_async_remote_copy(
            src_ref=src, dst_ref=dst, send_sem=ss, recv_sem=rs, device_id=to, device_id_type=MESH
        )

    def mod(v, n):
        return lax.rem(v + n, n)

    def half_of(which):
        return pl.ds(pl.multiple_of(which * half, HD), half)

    def q_rows(zz, xx, cc):
        return pl.ds(pl.multiple_of((zz * XN + xx) * (CORES * own) + cc * own, own), own)

    def q_pair(zz, xx):
        return pl.ds(pl.multiple_of((zz * XN + xx) * (CORES * own), CORES * own), CORES * own)

    k_own = pltpu.make_async_copy(k_ref.at[:, half_of(c)], k_buf.at[c], local_sem.at[0])
    v_own = pltpu.make_async_copy(v_ref.at[:, half_of(c)], v_buf.at[c], local_sem.at[1])
    q_own = pltpu.make_async_copy(q_ref.at[:, half_of(c)], q_all.at[q_rows(z, x, c)], local_sem.at[2])
    w_own = pltpu.make_async_copy(w_ref, w_in, local_sem.at[3])
    q_own.start()
    w_own.start()
    v_own.start()
    k_own.start()

    bar = pltpu.get_barrier_semaphore()

    def signal(to):
        pl.semaphore_signal(bar, inc=1, device_id=to, device_id_type=MESH)

    signals = 0
    for d in reversed(near_first(zn)):
        for cc in range(CORES):
            signal(dev(mod(z + d, zn), x, cc, y))
            signals += 1
    for d in reversed(near_first(yn)):
        for cc in range(CORES):
            signal(dev(z, x, cc, mod(y + d, yn)))
            signals += 1
    for d in near_first(XN):
        signal(dev(z, mod(x + d, XN), c, y))
        signals += 1
    signal(dev(z, x, sib, y))
    signals += 1

    top[...] = jnp.zeros_like(top)
    tot[...] = jnp.zeros_like(tot)

    for cb in range(CORES):
        hit = (pat_ref[...] == (z * XN + x) * CORES + cb).astype(F32)
        linked = jnp.max(hit, axis=1, keepdims=True)
        count = jnp.zeros((1, QB), F32)
        for b in range(nb):
            this = jnp.broadcast_to(linked[b : b + 1], (1, QB))
            for j in range(MOST):
                masks[b, cb * MOST + j : cb * MOST + j + 1, :] = jnp.where(count == j, this, 0.0)
            count = count + this
    pl.semaphore_wait(bar, signals)

    q_sib = remote(q_ref.at[:, half_of(sib)], q_all.at[q_rows(z, x, c)], qz_s.at[0, 0], qz_r.at[0, 0], dev(z, x, sib, y))
    q_sib.start()
    qz = {}
    for d in near_first(zn):
        for cc in range(CORES):
            copy = remote(
                q_ref.at[:, pl.ds(cc * half, half)],
                q_all.at[q_rows(z, x, c)],
                qz_s.at[d, cc],
                qz_r.at[d, c],
                dev(mod(z + d, zn), x, cc, y),
            )
            copy.start()
            qz[d, cc] = copy
    kv = [
        remote(ref.at[:, half_of(sib)], buf.at[c], kv_s.at[i], kv_r.at[i], dev(z, x, sib, y))
        for i, (ref, buf) in enumerate(((k_ref, k_buf), (v_ref, v_buf)))
    ]
    for copy in kv:
        copy.start()
    for d in range(1, yn):
        pl.semaphore_signal(ready, inc=1, device_id=dev(z, x, c, mod(y + d, yn)), device_id_type=MESH)

    def arrived(dst, sem):
        pltpu.make_async_copy(dst, dst, sem).wait()


    qx = []
    for n, d in enumerate([0] + near_first(zn)):
        zz = mod(z - d, zn)
        if d == 0:
            q_own.wait()
            arrived(q_all.at[q_rows(z, x, sib)], qz_r.at[0, 0])
        else:
            for cc in range(CORES):
                arrived(q_all.at[q_rows(zz, x, cc)], qz_r.at[d, cc])
        for e in near_first(XN):
            copy = remote(
                q_all.at[q_pair(zz, x)],
                q_all.at[q_pair(zz, x)],
                qx_s.at[d, e],
                qx_r.at[d, e],
                dev(z, mod(x + e, XN), c, y),
            )
            copy.start()
            qx.append(copy)
        if n == 0:
            w_own.wait()
            for cc in range(CORES):
                w_t[cc] = w_in[:, cc * half : (cc + 1) * half]
            w_all[y, c] = w_t[c]
            ws = [remote(w_t.at[sib], w_all.at[y, c], w_s.at[0, sib], w_r.at[0, c], dev(z, x, sib, y))]
            ws[0].start()
            for e in near_first(yn):
                for cc in range(CORES):
                    copy = remote(w_t.at[cc], w_all.at[y, c], w_s.at[e, cc], w_r.at[e, c], dev(z, x, cc, mod(y + e, yn)))
                    copy.start()
                    ws.append(copy)
            v_own.wait()
            for h in range(heads):
                v_t[c, h * HD : (h + 1) * HD, :] = v_buf[c, :, h * HD : (h + 1) * HD].T
    k_own.wait()
    for copy in kv:
        copy.wait_recv()
    for h in range(heads):
        v_t[sib, h * HD : (h + 1) * HD, :] = v_buf[sib, :, h * HD : (h + 1) * HD].T
    for d in [0] + near_first(zn):
        zz = mod(z - d, zn)
        for e in near_first(XN):
            arrived(q_all.at[q_pair(zz, mod(x - e, XN))], qx_r.at[d, e])

    scale = HD**-0.5 * math.log2(math.e)
    def choose(i, _):
        cb = i // MOST
        j = i % MOST
        mask = [masks[b, pl.ds(i, 1), :].astype(BF) for b in range(nb)]
        rows = pl.ds(pl.multiple_of(j * QB, QB), QB)
        for h in range(heads):
            cols = slice(h * HD, (h + 1) * HD)
            picked = [mask[b] * q_all[b * QB : (b + 1) * QB, cols] for b in range(nb)]
            q_sel[cb, h, rows, :] = functools.reduce(jnp.add, picked)
        return 0

    lax.fori_loop(0, CORES * MOST, choose, 0)

    def unit(i, _):
        cb = i // heads
        h = i % heads
        cols = pl.ds(pl.multiple_of(h * HD, HD), HD)
        k_h = k_buf[cb, :, cols]
        v_h = v_t[cb, cols, :]
        for p in range(MOST // 2):
            q_p = q_sel[cb, h, p * 2 * QB : (p + 1) * 2 * QB, :]
            s = lax.dot_general(k_h, q_p, NT, preferred_element_type=F32)
            m = jnp.max(s, axis=0, keepdims=True) * scale
            e = jnp.exp2(s * scale - m)
            l = jnp.sum(e, axis=0, keepdims=True)
            o = jnp.dot(v_h, e.astype(BF), preferred_element_type=F32)
            for t in range(2):
                j = p * 2 + t
                lanes = slice(t * QB, (t + 1) * QB)
                num[cb, j, cols, :] = o[:, lanes]
                top[cb, j, pl.ds(h, 1), :] = m[:, lanes]
                tot[cb, j, pl.ds(h, 1), :] = l[:, lanes]
        return 0

    lax.fori_loop(0, CORES * heads, unit, 0)

    row = lax.broadcasted_iota(jnp.int32, (8, QB), 0)

    def stats_of(m, l):
        high = l.astype(BF).astype(F32)
        first = jnp.where(row < heads, m, pltpu.roll(high, heads, 0))
        return jnp.concatenate([first, l - high], axis=0).astype(BF)

    def read_stats(block):
        block = block.astype(F32)
        first = block[0:8]
        return first, pltpu.roll(first, 8 - heads, 0) + block[8:16]

    rx = []
    for i in range(nb):
        b = mod(z - y + i + 1 + yn, nb)
        mask = masks[b]
        tops = [jnp.where(mask[i : i + 1] > 0.5, top[i // MOST, i % MOST], LOW) for i in range(CORES * MOST)]
        m = functools.reduce(jnp.maximum, tops).astype(BF).astype(F32)
        f = [jnp.exp2(t - m) for t in tops]
        stats = stats_of(m, functools.reduce(jnp.add, [f[i] * tot[i // MOST, i % MOST] for i in range(CORES * MOST)]))
        for h in range(heads):
            for xx in range(XN):
                rows = slice(h * HD + xx * dq, h * HD + (xx + 1) * dq)
                terms = [f[i][h : h + 1] * num[i // MOST, i % MOST, rows, :] for i in range(CORES * MOST)]
                parts[xx, b, h * dq : (h + 1) * dq, :] = functools.reduce(jnp.add, terms).astype(BF)
        for xx in range(XN):
            parts[xx, b, body:, :] = stats
        for e in near_first(XN):
            to = mod(x + e, XN)
            copy = remote(parts.at[to, b], parts_in.at[e, b], rx_s.at[e, i], rx_r.at[e, i], dev(z, to, c, y))
            copy.start()
            rx.append(copy)

    def merge(blocks):
        stats = [read_stats(block[body:, :]) for block in blocks]
        m = functools.reduce(jnp.maximum, [s[0] for s in stats])
        factors = [jnp.exp2(s[0] - m) for s in stats]
        l = functools.reduce(jnp.add, [f * s[1] for f, s in zip(factors, stats)])
        sums_of = []
        for h in range(heads):
            rows = slice(h * dq, (h + 1) * dq)
            sums_of.append(
                functools.reduce(
                    jnp.add, [f[h : h + 1] * block[rows, :].astype(F32) for f, block in zip(factors, blocks)]
                )
            )
        return sums_of, m, l

    pl.semaphore_wait(ready, yn - 1)
    for i in range(nb):
        b = mod(z - y + i + 1 + yn, nb)
        for e in near_first(XN):
            arrived(parts_in.at[e, b], rx_r.at[e, i])
        merged, m, l = merge([parts.at[x, b]] + [parts_in.at[e, b] for e in near_first(XN)])
        for h in range(heads):
            sums[i, h * dq : (h + 1) * dq, :] = merged[h].astype(BF)
        sums[i, body:, :] = stats_of(m, l)
        zz = mod(z + i + 1, zn)
        here = jnp.logical_and(zz == z, b == y)

        @pl.when(here)
        def _():
            pltpu.make_async_copy(sums.at[i], sums_in.at[z], rz_r.at[z]).start()

        @pl.when(jnp.logical_not(here))
        def _():
            remote(sums.at[i], sums_in.at[z], rz_s.at[i], rz_r.at[z], dev(zz, x, c, b)).start()

    for zz in range(zn):
        arrived(sums_in.at[zz], rz_r.at[zz])
    merged, m, l = merge([sums_in.at[zz] for zz in range(zn)])
    for h in range(heads):
        att[z, x, h * dq : (h + 1) * dq, :] = (merged[h] / l[h : h + 1]).astype(BF)

    def rz_wait():
        for i in range(nb):
            b = mod(z - y + i + 1 + yn, nb)
            here = jnp.logical_and(mod(z + i + 1, zn) == z, b == y)

            @pl.when(jnp.logical_not(here))
            def _():
                remote(sums.at[i], sums_in.at[z], rz_s.at[i], rz_r.at[z], dev(z, x, c, y)).wait_send()

    az, ax = [], []
    for d in near_first(zn):
        copy = remote(att.at[z, x], att.at[z, x], az_s.at[d], az_r.at[d], dev(mod(z + d, zn), x, c, y))
        copy.start()
        az.append(copy)
    for d in [0] + near_first(zn):
        zz = mod(z - d, zn)
        if d:
            arrived(att.at[zz, x], az_r.at[d])
        for e in near_first(XN):
            copy = remote(att.at[zz, x], att.at[zz, x], ax_s.at[d, e], ax_r.at[d, e], dev(z, mod(x + e, XN), c, y))
            copy.start()
            ax.append(copy)

    arrived(w_all.at[y, sib], w_r.at[0, sib])
    for e in near_first(yn):
        for cc in range(CORES):
            arrived(w_all.at[mod(y - e, yn), cc], w_r.at[e, cc])
    total = None
    for d in [0] + near_first(zn):
        zz = mod(z - d, zn)
        for e in near_first(XN):
            arrived(att.at[zz, mod(x - e, XN)], ax_r.at[d, e])
        yy = mod(zz - y, yn)
        wide = w_all[yy].reshape(CORES * w_all.shape[2], half)
        rows = jnp.concatenate(
            [att[zz, xx, h * dq : (h + 1) * dq, :] for h in range(heads) for xx in range(XN)], axis=0
        )
        term = jnp.dot(wide, rows, preferred_element_type=F32)
        total = term if total is None else total + term
    acc[...] = total.reshape(acc.shape)
    last = remote(acc.at[sib], acc_in, sib_s, sib_r, dev(z, x, sib, y))
    last.start()
    q_sib.wait_send()
    for group in (qz.values(), qx, kv, ws, rx, az, ax):
        for copy in group:
            copy.wait_send()
    rz_wait()
    last.wait()
    out_ref[...] = (acc[c] + acc_in[...]).astype(BF)


def shards(queries, keys, values, pattern, out_weight):
    yn = lax.axis_size("heads")
    zn = lax.axis_size("rows") // (XN * CORES)
    nb = pattern.shape[0]
    own, width = queries.shape
    half = width // CORES
    heads = half // HD
    cblk = keys.shape[0]
    cols = out_weight.shape[1]
    piece = heads * (HD // XN)
    load = piece + STATS
    dma = pltpu.SemaphoreType.DMA
    anywhere = pl.BlockSpec(memory_space=pl.ANY)
    return pl.pallas_call(
        kernel,
        name="attend_project",
        out_shape=jax.ShapeDtypeStruct((cols, QB), BF),
        in_specs=[anywhere, anywhere, anywhere, pl.BlockSpec(memory_space=pltpu.VMEM), anywhere],
        out_specs=pl.BlockSpec(memory_space=pltpu.VMEM),
        scratch_shapes=[
            pltpu.VMEM((nb * QB, half), BF),
            pltpu.VMEM((CORES, cblk, half), BF),
            pltpu.VMEM((CORES, cblk, half), BF),
            pltpu.VMEM((CORES, half, cblk), BF),
            pltpu.VMEM((cols, width), BF),
            pltpu.VMEM((CORES, cols, half), BF),
            pltpu.VMEM((yn, CORES, cols, half), BF),
            pltpu.VMEM((CORES, heads, MOST * QB, HD), BF),
            pltpu.VMEM((CORES, MOST, half, QB), F32),
            pltpu.VMEM((CORES, MOST, 8, QB), F32),
            pltpu.VMEM((CORES, MOST, 8, QB), F32),
            pltpu.VMEM((XN, nb, load, QB), BF),
            pltpu.VMEM((XN, nb, load, QB), BF),
            pltpu.VMEM((nb, load, QB), BF),
            pltpu.VMEM((zn, load, QB), BF),
            pltpu.VMEM((zn, XN, piece, QB), BF),
            pltpu.VMEM((CORES, cols, QB), F32),
            pltpu.VMEM((cols, QB), F32),
            pltpu.VMEM((nb, CORES * MOST, QB), F32),
            dma((4,)),
            dma((zn, CORES)),
            dma((zn, CORES)),
            dma((zn, XN)),
            dma((zn, XN)),
            dma((2,)),
            dma((2,)),
            dma((yn, CORES)),
            dma((yn, CORES)),
            dma((XN, nb)),
            dma((XN, nb)),
            dma((nb,)),
            dma((zn,)),
            dma((zn,)),
            dma((zn,)),
            dma((zn, XN)),
            dma((zn, XN)),
            dma,
            dma,
            pltpu.SemaphoreType.REGULAR,
        ],
        compiler_params=pltpu.CompilerParams(
            collective_id=0, has_side_effects=True, vmem_limit_bytes=64 * 2**20
        ),
        cost_estimate=pl.CostEstimate(flops=3 * 10**9, bytes_accessed=4 * 10**6, transcendentals=3 * 10**6),
    )(queries, keys, values, pattern, out_weight.T).T


def solution(mesh):
    in_specs = (P("rows", "heads"), P("rows", "heads"), P("rows", "heads"), P(), P("heads", "rows"))
    out_specs = P("heads", "rows")
    return jax.shard_map(shards, mesh=mesh, in_specs=in_specs, out_specs=out_specs, check_vma=False)
```

```python
import functools
import math

import jax
import jax.numpy as jnp
from jax import lax
from jax.experimental import pallas as pl
from jax.experimental.pallas import tpu as pltpu
from jax.sharding import PartitionSpec as P

MESH = pl.DeviceIdType.MESH
HD = 128
QB = 128
MOST = 4
CORES = 2
XN = 4
STATS = 16
LANES = 128
LOW = -(2.0**100)
NT = (((1,), (1,)), ((), ()))
BF = jnp.bfloat16
F32 = jnp.float32


def near_first(n):
    order = []
    for step in range(1, n // 2 + 1):
        order.append(step)
        if n - step != step:
            order.append(n - step)
    return order


def kernel(
    q_ref,
    k_ref,
    v_ref,
    pat_ref,
    w_ref,
    out_ref,
    q_all,
    k_buf,
    v_buf,
    v_t,
    w_in,
    w_piece,
    w_mine,
    w_wide,
    w_all,
    w_turned,
    q_sel,
    score,
    peak,
    num,
    top,
    tot,
    parts,
    parts_in,
    ends,
    ends_in,
    weight,
    stat_m,
    stat_l,
    sums,
    sums_in,
    att,
    out_part,
    out_in,
    masks,
    local_sem,
    qz_s,
    qz_r,
    qx_s,
    qx_r,
    kv_s,
    kv_r,
    wx_s,
    wx_r,
    wy_s,
    wy_r,
    qh_s,
    qh_r,
    rx_s,
    rx_r,
    rz_s,
    rz_r,
    az_s,
    az_r,
    out_s,
    out_r,
    ready,
):
    r = lax.axis_index("rows")
    y = lax.axis_index("heads")
    yn = w_all.shape[0]
    zn = att.shape[0]
    nb = zn
    heads = num.shape[2] // HD
    half = heads * HD
    dq = HD // XN
    body = heads * dq
    own = q_ref.shape[0]
    z = r // (XN * CORES)
    x = (r // CORES) % XN
    c = r % CORES
    sib = 1 - c

    def dev(dz, dx, dc, dy):
        return ((dz * XN + dx) * CORES + dc, dy)

    def remote(src, dst, ss, rs, to):
        return pltpu.make_async_remote_copy(
            src_ref=src, dst_ref=dst, send_sem=ss, recv_sem=rs, device_id=to, device_id_type=MESH
        )

    def mod(v, n):
        return lax.rem(v + n, n)

    def half_of(which):
        return pl.ds(pl.multiple_of(which * half, HD), half)

    def q_rows(zz, xx, cc):
        return pl.ds(pl.multiple_of((zz * XN + xx) * (CORES * own) + cc * own, own), own)

    def q_pair(zz, xx):
        return pl.ds(pl.multiple_of((zz * XN + xx) * (CORES * own), CORES * own), CORES * own)

    k_own = pltpu.make_async_copy(k_ref.at[:, half_of(c)], k_buf.at[c], local_sem.at[0])
    v_own = pltpu.make_async_copy(v_ref.at[:, half_of(c)], v_buf.at[c], local_sem.at[1])
    q_own = pltpu.make_async_copy(q_ref.at[:, half_of(c)], q_all.at[q_rows(z, x, c)], local_sem.at[2])
    w_own = pltpu.make_async_copy(w_ref, w_in.at[0 : w_ref.shape[0]], local_sem.at[3])
    q_own.start()
    w_own.start()
    v_own.start()
    k_own.start()

    bar = pltpu.get_barrier_semaphore()

    def signal(to):
        pl.semaphore_signal(bar, inc=1, device_id=to, device_id_type=MESH)

    near = (1, -1, 2, -2)
    far = ((2, (-1, -2)), (-2, (1,)))
    onward = {2: (1, 2), -2: (-1,)}
    group = [(e, f) for e in (2, 1, 3, 0) for f in (1, 0) if e or f]
    for d in reversed(near_first(zn)):
        signal(dev(mod(z + d, zn), x, c, y))
    for d in reversed(near_first(yn)):
        signal(dev(z, x, c, mod(y + d, yn)))
    for e, f in group:
        signal(dev(z, mod(x + e, XN), mod(c + f, CORES), y))
    signals = zn - 1 + yn - 1 + len(group)

    pl.semaphore_wait(bar, signals)

    q_sib = remote(q_ref.at[:, half_of(sib)], q_all.at[q_rows(z, x, c)], qz_s.at[0], qz_r.at[0], dev(z, x, sib, y))
    q_sib.start()

    def arrived(dst, sem):
        pltpu.make_async_copy(dst, dst, sem).wait()

    q_own.wait()
    arrived(q_all.at[q_rows(z, x, sib)], qz_r.at[0])

    def along_z(ref, origin, hop, distance, ss, rs):
        copy = remote(ref, ref, ss.at[distance % zn], rs.at[distance % zn], dev(mod(z + hop, zn), x, c, y))
        copy.start()
        return copy

    def pair_from(d):
        return q_all.at[q_pair(mod(z - d, zn), x)]

    qz, qx = [], []

    def along_x(d):
        for e in near_first(XN):
            pair = pair_from(d)
            copy = remote(pair, pair, qx_s.at[d % zn, e], qx_r.at[d % zn, e], dev(z, mod(x + e, XN), c, y))
            copy.start()
            qx.append(copy)

    for d in near:
        qz.append(along_z(pair_from(0), 0, d, d, qz_s, qz_r))
    along_x(0)
    kv = [
        remote(ref.at[:, half_of(sib)], buf.at[c], kv_s.at[i], kv_r.at[i], dev(z, x, sib, y))
        for i, (ref, buf) in enumerate(((k_ref, k_buf), (v_ref, v_buf)))
    ]
    for copy in kv:
        copy.start()
    for d in range(1, yn):
        pl.semaphore_signal(ready, inc=1, device_id=dev(z, x, c, mod(y + d, yn)), device_id_type=MESH)

    w_in[w_ref.shape[0] :, :] = jnp.zeros((LANES - w_ref.shape[0], w_in.shape[1]), BF)
    w_own.wait()
    for cc in range(CORES):
        for h in range(heads):
            first = cc * half + h * HD
            turned = w_in[:, first : first + HD].astype(F32).T.astype(BF)
            for xx in range(XN):
                w_piece[xx, cc, h * dq : (h + 1) * dq, :] = turned[xx * dq : (xx + 1) * dq]
    w_mine[x, c] = w_piece[x, c]
    wx = []
    for e, f in group:
        to = mod(x + e, XN), mod(c + f, CORES)
        copy = remote(w_piece.at[to[0], to[1]], w_mine.at[x, c], wx_s.at[e, f], wx_r.at[e, f], dev(z, to[0], to[1], y))
        copy.start()
        wx.append(copy)

    top[...] = jnp.zeros_like(top)
    tot[...] = jnp.zeros_like(tot)
    stat_m[...] = jnp.zeros_like(stat_m)
    stat_l[...] = jnp.zeros_like(stat_l)

    for cb in range(CORES):
        hit = (pat_ref[...] == (z * XN + x) * CORES + cb).astype(F32)
        linked = jnp.max(hit, axis=1, keepdims=True)
        count = jnp.zeros((1, QB), F32)
        for b in range(nb):
            this = jnp.broadcast_to(linked[b : b + 1], (1, QB))
            for j in range(MOST):
                masks[b, cb * MOST + j : cb * MOST + j + 1, :] = jnp.where(count == j, this, 0.0)
            count = count + this
    for d in (2, -2, 1, -1):
        arrived(pair_from(d), qz_r.at[d % zn])
        for hop in onward.get(d, ()):
            qz.append(along_z(pair_from(d), d, hop, d + hop, qz_s, qz_r))
        along_x(d)

    for e, f in group:
        arrived(w_mine.at[mod(x - e, XN), mod(c - f, CORES)], wx_r.at[e, f])
    cols = out_ref.shape[0]
    every = [w_mine[xx, cc][:, 0:cols] for xx in range(XN) for cc in range(CORES)]
    w_wide[...] = jnp.concatenate(every, axis=1)
    wy = []

    def weights(src, origin, to, which):
        copy = remote(src, w_all.at[mod(origin + to + yn, yn)], wy_s.at[which], wy_r.at[which], dev(z, x, c, mod(to + yn, yn)))
        copy.start()
        wy.append(copy)

    for d in near:
        weights(w_wide, y, y + d, d % yn)
    w_all[mod(y + y, yn)] = w_wide[...]
    distant = (3, -3, 4)
    for d in distant:
        arrived(pair_from(d), qz_r.at[d % zn])

    def head_of(d, xx, h):
        return q_all.at[q_pair(mod(z - d, zn), xx), pl.ds(h * HD, HD)]

    for h in range(heads):
        for n, d in enumerate(distant):
            for e in near_first(XN):
                mine = head_of(d, x, h)
                copy = remote(mine, mine, qh_s.at[h, n, e], qh_r.at[h, n, e], dev(z, mod(x + e, XN), c, y))
                copy.start()
                qx.append(copy)
    v_own.wait()
    for h in range(heads):
        v_t[c, h * HD : (h + 1) * HD, :] = v_buf[c, :, h * HD : (h + 1) * HD].T
    k_own.wait()
    for copy in kv:
        copy.wait_recv()
    for h in range(heads):
        v_t[sib, h * HD : (h + 1) * HD, :] = v_buf[sib, :, h * HD : (h + 1) * HD].T
    for d in (0,) + near:
        for e in near_first(XN):
            arrived(q_all.at[q_pair(mod(z - d, zn), mod(x - e, XN))], qx_r.at[d % zn, e])

    scale = HD**-0.5 * math.log2(math.e)

    def choose(h):
        for n, d in enumerate(distant):
            for e in near_first(XN):
                arrived(head_of(d, mod(x - e, XN), h), qh_r.at[h, n, e])
        cols = slice(h * HD, (h + 1) * HD)

        def slot(i, _):
            rows = pl.ds(pl.multiple_of((i % MOST) * QB, QB), QB)
            picked = [masks[b, pl.ds(i, 1), :].astype(BF) * q_all[b * QB : (b + 1) * QB, cols] for b in range(nb)]
            q_sel[i // MOST, h, rows, :] = functools.reduce(jnp.add, picked)
            return 0

        lax.fori_loop(0, CORES * MOST, slot, 0)

    def front(h, cb):
        cols = slice(h * HD, (h + 1) * HD)
        s = lax.dot_general(k_buf[cb, :, cols], q_sel[cb, h], NT, preferred_element_type=F32)
        score[cb] = s
        peak[cb] = jnp.broadcast_to(jnp.max(s, axis=0, keepdims=True) * scale, (8, MOST * QB))

    def back(h, cb):
        cols = slice(h * HD, (h + 1) * HD)
        m = peak[cb, 0:1]
        e = jnp.exp2(score[cb] * scale - m)
        l = jnp.sum(e, axis=0, keepdims=True)
        o = jnp.dot(v_t[cb, cols, :], e.astype(BF), preferred_element_type=F32)
        for j in range(MOST):
            lanes = slice(j * QB, (j + 1) * QB)
            num[cb, j, cols, :] = o[:, lanes]
            top[cb, j, h : h + 1, :] = m[:, lanes]
            tot[cb, j, h : h + 1, :] = l[:, lanes]

    row = lax.broadcasted_iota(jnp.int32, (8, QB), 0)

    def stats_of(m, l):
        high = l.astype(BF).astype(F32)
        first = jnp.where(row < heads, m, pltpu.roll(high, heads, 0))
        return jnp.concatenate([first, l - high], axis=0).astype(BF)

    def read_stats(block):
        block = block.astype(F32)
        first = block[0:8]
        return first, pltpu.roll(first, 8 - heads, 0) + block[8:16]

    rx = []
    slots = range(CORES * MOST)

    def turn(i):
        return mod(z - y + i + 1 + yn, nb)

    def partial(h, b, xx):
        f = weight[b, h]
        rows = slice(h * HD + xx * dq, h * HD + (xx + 1) * dq)
        terms = [f[i : i + 1] * num[i // MOST, i % MOST, rows, :] for i in slots]
        return functools.reduce(jnp.add, terms).astype(BF)

    def weigh(h, b):
        mask = masks[b]
        tops = jnp.concatenate([top[i // MOST, i % MOST, h : h + 1, :] for i in slots], axis=0)
        tots = jnp.concatenate([tot[i // MOST, i % MOST, h : h + 1, :] for i in slots], axis=0)
        tops = jnp.where(mask > 0.5, tops, LOW)
        m = jnp.max(tops, axis=0, keepdims=True).astype(BF).astype(F32)
        f = jnp.exp2(tops - m)
        weight[b, h] = f
        stat_m[b, h : h + 1, :] = m
        stat_l[b, h : h + 1, :] = jnp.sum(f * tots, axis=0, keepdims=True)

    choose(0)
    front(0, 0)
    for h in range(heads):
        front(h, 1)
        back(h, 0)
        if h + 1 < heads:
            choose(h + 1)
            front(h + 1, 0)
        back(h, 1)
        if h + 1 < heads:

            def whole(b, _):
                weigh(h, b)
                for xx in range(XN):
                    parts[xx, h, b] = partial(h, b, xx)
                return 0

            lax.fori_loop(0, nb, whole, 0)
            for e in near_first(XN):
                to = mod(x + e, XN)
                copy = remote(parts.at[to, h], parts_in.at[e, h], rx_s.at[e, nb + h], rx_r.at[e, nb + h], dev(z, to, c, y))
                copy.start()
                rx.append(copy)
        if h == 0:
            for d, hops in far:
                origin = y + d
                arrived(w_all.at[mod(y + origin + yn, yn)], wy_r.at[-d % yn])
                for hop in hops:
                    weights(w_all.at[mod(origin + y + yn, yn)], origin, y + hop, (hop - d) % yn)

    for i in range(nb):
        b = turn(i)
        weigh(heads - 1, b)
        stats = stats_of(stat_m[b], stat_l[b])
        for xx in range(XN):
            ends[xx, b, 0:dq, :] = partial(heads - 1, b, xx)
            ends[xx, b, dq:, :] = stats
        for e in near_first(XN):
            to = mod(x + e, XN)
            copy = remote(ends.at[to, b], ends_in.at[e, b], rx_s.at[e, i], rx_r.at[e, i], dev(z, to, c, y))
            copy.start()
            rx.append(copy)

    def merge(all_stats, blocks):
        stats = [read_stats(block) for block in all_stats]
        m = functools.reduce(jnp.maximum, [s[0] for s in stats])
        factors = [jnp.exp2(s[0] - m) for s in stats]
        l = functools.reduce(jnp.add, [f * s[1] for f, s in zip(factors, stats)])
        sums_of = []
        for h in range(heads):
            terms = [f[h : h + 1] * block.astype(F32) for f, block in zip(factors, blocks[h])]
            sums_of.append(functools.reduce(jnp.add, terms))
        return sums_of, m, l

    pl.semaphore_wait(ready, yn - 1)
    for h in range(heads - 1):
        for e in near_first(XN):
            arrived(parts_in.at[e, h], rx_r.at[e, nb + h])
    for i in range(nb):
        b = turn(i)
        for e in near_first(XN):
            arrived(ends_in.at[e, b], rx_r.at[e, i])
        blocks = [[parts[x, h, b]] + [parts_in[e, h, b] for e in near_first(XN)] for h in range(heads - 1)]
        got = [ends[x, b]] + [ends_in[e, b] for e in near_first(XN)]
        blocks.append([block[0:dq] for block in got])
        merged, m, l = merge([block[dq:] for block in got], blocks)
        for h in range(heads):
            sums[i, h * dq : (h + 1) * dq, :] = merged[h].astype(BF)
        sums[i, body:, :] = stats_of(m, l)
        zz = mod(z + i + 1, zn)
        here = jnp.logical_and(zz == z, b == y)

        @pl.when(here)
        def _():
            pltpu.make_async_copy(sums.at[i], sums_in.at[z], rz_r.at[z]).start()

        @pl.when(jnp.logical_not(here))
        def _():
            remote(sums.at[i], sums_in.at[z], rz_s.at[i], rz_r.at[z], dev(zz, x, c, b)).start()

    for zz in range(zn):
        arrived(sums_in.at[zz], rz_r.at[zz])
    got = [sums_in[zz] for zz in range(zn)]
    blocks = [[block[h * dq : (h + 1) * dq] for block in got] for h in range(heads)]
    merged, m, l = merge([block[body:] for block in got], blocks)
    for h in range(heads):
        att[z, h * dq : (h + 1) * dq, :] = (merged[h] / l[h : h + 1]).astype(BF)

    def rz_wait():
        for i in range(nb):
            b = turn(i)
            here = jnp.logical_and(mod(z + i + 1, zn) == z, b == y)

            @pl.when(jnp.logical_not(here))
            def _():
                remote(sums.at[i], sums_in.at[z], rz_s.at[i], rz_r.at[z], dev(z, x, c, y)).wait_send()

    az = [along_z(att.at[z], 0, d, d, az_s, az_r) for d in near]
    for d in (2, -2):
        piece = att.at[mod(z - d, zn)]
        arrived(piece, az_r.at[d % zn])
        for hop in onward[d]:
            az.append(along_z(piece, d, hop, d + hop, az_s, az_r))
    for d in range(1, yn):
        if d not in (2, yn - 2):
            arrived(w_all.at[mod(y + y - d + yn, yn)], wy_r.at[d])
    w_turned[...] = w_all[...].reshape(zn * body, w_all.shape[2]).T
    for d in (1, -1, 3, -3, 4):
        arrived(att.at[mod(z - d, zn)], az_r.at[d % zn])

    rows = att[...].reshape(zn * body, QB)
    outs = []
    for e, f in group + [(0, 0)]:
        xx, cc = mod(x + e, XN), mod(c + f, CORES)
        wide = w_turned[pl.ds(pl.multiple_of((xx * CORES + cc) * cols, cols), cols), :]
        term = jnp.dot(wide, rows, preferred_element_type=F32)
        if e or f:
            out_part[xx, cc] = term.astype(BF)
            copy = remote(out_part.at[xx, cc], out_in.at[e, f], out_s.at[e, f], out_r.at[e, f], dev(z, xx, cc, y))
            copy.start()
            outs.append(copy)
    for sent in ([q_sib], qz, qx, kv, wx, wy, rx, az):
        for copy in sent:
            copy.wait_send()
    rz_wait()
    for copy in outs:
        copy.wait()
    for e, f in group:
        term = term + out_in[e, f].astype(F32)
    out_ref[...] = term.astype(BF)


def shards(queries, keys, values, pattern, out_weight):
    yn = lax.axis_size("heads")
    zn = lax.axis_size("rows") // (XN * CORES)
    nb = pattern.shape[0]
    own, width = queries.shape
    half = width // CORES
    heads = half // HD
    cblk = keys.shape[0]
    cols = out_weight.shape[1]
    piece = heads * (HD // XN)
    load = piece + STATS
    dma = pltpu.SemaphoreType.DMA
    anywhere = pl.BlockSpec(memory_space=pl.ANY)
    return pl.pallas_call(
        kernel,
        name="attend_project",
        out_shape=jax.ShapeDtypeStruct((cols, QB), BF),
        in_specs=[anywhere, anywhere, anywhere, pl.BlockSpec(memory_space=pltpu.VMEM), anywhere],
        out_specs=pl.BlockSpec(memory_space=pltpu.VMEM),
        scratch_shapes=[
            pltpu.VMEM((nb * QB, half), BF),
            pltpu.VMEM((CORES, cblk, half), BF),
            pltpu.VMEM((CORES, cblk, half), BF),
            pltpu.VMEM((CORES, half, cblk), BF),
            pltpu.VMEM((LANES, width), BF),
            pltpu.VMEM((XN, CORES, piece, LANES), BF),
            pltpu.VMEM((XN, CORES, piece, LANES), BF),
            pltpu.VMEM((piece, XN * CORES * cols), BF),
            pltpu.VMEM((yn, piece, XN * CORES * cols), BF),
            pltpu.VMEM((XN * CORES * cols, zn * piece), BF),
            pltpu.VMEM((CORES, heads, MOST * QB, HD), BF),
            pltpu.VMEM((2, cblk, MOST * QB), F32),
            pltpu.VMEM((2, 8, MOST * QB), F32),
            pltpu.VMEM((CORES, MOST, half, QB), F32),
            pltpu.VMEM((CORES, MOST, 8, QB), F32),
            pltpu.VMEM((CORES, MOST, 8, QB), F32),
            pltpu.VMEM((XN, heads - 1, nb, HD // XN, QB), BF),
            pltpu.VMEM((XN, heads - 1, nb, HD // XN, QB), BF),
            pltpu.VMEM((XN, nb, HD // XN + STATS, QB), BF),
            pltpu.VMEM((XN, nb, HD // XN + STATS, QB), BF),
            pltpu.VMEM((nb, heads, CORES * MOST, QB), F32),
            pltpu.VMEM((nb, 8, QB), F32),
            pltpu.VMEM((nb, 8, QB), F32),
            pltpu.VMEM((nb, load, QB), BF),
            pltpu.VMEM((zn, load, QB), BF),
            pltpu.VMEM((zn, piece, QB), BF),
            pltpu.VMEM((XN, CORES, cols, QB), BF),
            pltpu.VMEM((XN, CORES, cols, QB), BF),
            pltpu.VMEM((nb, CORES * MOST, QB), F32),
            dma((4,)),
            dma((zn,)),
            dma((zn,)),
            dma((zn, XN)),
            dma((zn, XN)),
            dma((2,)),
            dma((2,)),
            dma((XN, CORES)),
            dma((XN, CORES)),
            dma((yn,)),
            dma((yn,)),
            dma((heads, 3, XN)),
            dma((heads, 3, XN)),
            dma((XN, nb + heads - 1)),
            dma((XN, nb + heads - 1)),
            dma((nb,)),
            dma((zn,)),
            dma((zn,)),
            dma((zn,)),
            dma((XN, CORES)),
            dma((XN, CORES)),
            pltpu.SemaphoreType.REGULAR,
        ],
        compiler_params=pltpu.CompilerParams(
            collective_id=0, has_side_effects=True, vmem_limit_bytes=64 * 2**20
        ),
        cost_estimate=pl.CostEstimate(flops=3 * 10**9, bytes_accessed=4 * 10**6, transcendentals=3 * 10**6),
    )(queries, keys, values, pattern, out_weight.T).T


def solution(mesh):
    in_specs = (P("rows", "heads"), P("rows", "heads"), P("rows", "heads"), P(), P("heads", "rows"))
    out_specs = P("heads", "rows")
    return jax.shard_map(shards, mesh=mesh, in_specs=in_specs, out_specs=out_specs, check_vma=False)
```

```python
import functools
import math

import jax
import jax.numpy as jnp
from jax import lax
from jax.experimental import pallas as pl
from jax.experimental.pallas import tpu as pltpu
from jax.sharding import PartitionSpec as P

MESH = pl.DeviceIdType.MESH
HD = 128
QB = 128
MOST = 4
CORES = 2
XN = 4
STATS = 16
LANES = 128
LOW = -(2.0**100)
NT = (((1,), (1,)), ((), ()))
BF = jnp.bfloat16
F32 = jnp.float32


def near_first(n):
    order = []
    for step in range(1, n // 2 + 1):
        order.append(step)
        if n - step != step:
            order.append(n - step)
    return order


def kernel(
    q_ref,
    k_ref,
    v_ref,
    pat_ref,
    w_ref,
    out_ref,
    q_all,
    k_buf,
    v_buf,
    v_t,
    w_in,
    w_piece,
    w_mine,
    w_wide,
    w_all,
    w_turned,
    q_sel,
    score,
    peak,
    num,
    top,
    tot,
    parts,
    parts_in,
    ends,
    ends_in,
    weight,
    stat_m,
    stat_l,
    sums,
    sums_in,
    att,
    out_part,
    out_in,
    masks,
    local_sem,
    qz_s,
    qz_r,
    qx_s,
    qx_r,
    kv_s,
    kv_r,
    wx_s,
    wx_r,
    wy_s,
    wy_r,
    qh_s,
    qh_r,
    rx_s,
    rx_r,
    rz_s,
    rz_r,
    az_s,
    az_r,
    out_s,
    out_r,
    ready,
    ready_all,
):
    r = lax.axis_index("rows")
    y = lax.axis_index("heads")
    yn = w_all.shape[0]
    zn = att.shape[0]
    nb = zn
    heads = num.shape[2] // HD
    half = heads * HD
    dq = HD // XN
    body = heads * dq
    own = q_ref.shape[0]
    z = r // (XN * CORES)
    x = (r // CORES) % XN
    c = r % CORES
    sib = 1 - c

    def dev(dz, dx, dc, dy):
        return ((dz * XN + dx) * CORES + dc, dy)

    def remote(src, dst, ss, rs, to):
        return pltpu.make_async_remote_copy(
            src_ref=src, dst_ref=dst, send_sem=ss, recv_sem=rs, device_id=to, device_id_type=MESH
        )

    def mod(v, n):
        return lax.rem(v + n, n)

    def half_of(which):
        return pl.ds(pl.multiple_of(which * half, HD), half)

    def q_rows(zz, xx, cc):
        return pl.ds(pl.multiple_of((zz * XN + xx) * (CORES * own) + cc * own, own), own)

    def q_pair(zz, xx):
        return pl.ds(pl.multiple_of((zz * XN + xx) * (CORES * own), CORES * own), CORES * own)

    k_own = pltpu.make_async_copy(k_ref.at[:, half_of(c)], k_buf.at[c], local_sem.at[0])
    v_own = pltpu.make_async_copy(v_ref.at[:, half_of(c)], v_buf.at[c], local_sem.at[1])
    q_own = pltpu.make_async_copy(q_ref.at[:, half_of(c)], q_all.at[q_rows(z, x, c)], local_sem.at[2])
    w_own = pltpu.make_async_copy(w_ref, w_in.at[0 : w_ref.shape[0]], local_sem.at[3])
    q_own.start()
    w_own.start()
    v_own.start()
    k_own.start()

    bar = pltpu.get_barrier_semaphore()

    def signal(to):
        pl.semaphore_signal(bar, inc=1, device_id=to, device_id_type=MESH)

    near = (1, -1, 2, -2)
    far = ((2, (-1, -2)), (-2, (1,)))
    onward = {2: (1, 2), -2: (-1,)}
    group = [(e, f) for e in (2, 1, 3, 0) for f in (1, 0) if e or f]
    for d in reversed(near):
        for cc in range(CORES):
            signal(dev(mod(z + d, zn), x, cc, y))
        signal(dev(z, x, c, mod(y + d, yn)))
    for e, f in group:
        signal(dev(z, mod(x + e, XN), mod(c + f, CORES), y))
    signals = len(near) * (CORES + 1) + len(group)

    pl.semaphore_wait(bar, signals)

    rows_here = q_all.at[q_rows(z, x, c)]
    qz, qx = [], []

    def half_to(cc, d, ss):
        copy = remote(q_ref.at[:, half_of(cc)], rows_here, ss, qz_r.at[d % zn, c], dev(mod(z + d, zn), x, cc, y))
        copy.start()
        qz.append(copy)

    half_to(sib, 0, qz_s.at[0, 0])
    for d in near:
        for cc in range(CORES):
            half_to(cc, d, qz_s.at[d % zn, cc])

    def arrived(dst, sem):
        pltpu.make_async_copy(dst, dst, sem).wait()

    def along_z(ref, origin, hop, distance, ss, rs):
        copy = remote(ref, ref, ss(distance % zn), rs(distance % zn), dev(mod(z + hop, zn), x, c, y))
        copy.start()
        return copy

    def pair_from(d):
        return q_all.at[q_pair(mod(z - d, zn), x)]


    def along_x(d):
        for e in near_first(XN):
            pair = pair_from(d)
            copy = remote(pair, pair, qx_s.at[d % zn, e], qx_r.at[d % zn, e], dev(z, mod(x + e, XN), c, y))
            copy.start()
            qx.append(copy)

    q_own.wait()
    arrived(q_all.at[q_rows(z, x, sib)], qz_r.at[0, sib])
    along_x(0)
    kv = [
        remote(ref.at[:, half_of(sib)], buf.at[c], kv_s.at[i], kv_r.at[i], dev(z, x, sib, y))
        for i, (ref, buf) in enumerate(((k_ref, k_buf), (v_ref, v_buf)))
    ]
    for copy in kv:
        copy.start()

    w_in[w_ref.shape[0] :, :] = jnp.zeros((LANES - w_ref.shape[0], w_in.shape[1]), BF)
    w_own.wait()
    for cc in range(CORES):
        for h in range(heads):
            first = cc * half + h * HD
            turned = w_in[:, first : first + HD].astype(F32).T.astype(BF)
            for xx in range(XN):
                w_piece[xx, cc, h * dq : (h + 1) * dq, :] = turned[xx * dq : (xx + 1) * dq]
    w_mine[x, c] = w_piece[x, c]
    wx = []
    for e, f in group:
        to = mod(x + e, XN), mod(c + f, CORES)
        copy = remote(w_piece.at[to[0], to[1]], w_mine.at[x, c], wx_s.at[e, f], wx_r.at[e, f], dev(z, to[0], to[1], y))
        copy.start()
        wx.append(copy)

    top[...] = jnp.zeros_like(top)
    tot[...] = jnp.zeros_like(tot)
    stat_m[...] = jnp.zeros_like(stat_m)
    stat_l[...] = jnp.zeros_like(stat_l)

    for cb in range(CORES):
        hit = (pat_ref[...] == (z * XN + x) * CORES + cb).astype(F32)
        linked = jnp.max(hit, axis=1, keepdims=True)
        count = jnp.zeros((1, QB), F32)
        for b in range(nb):
            this = jnp.broadcast_to(linked[b : b + 1], (1, QB))
            for j in range(MOST):
                masks[b, cb * MOST + j : cb * MOST + j + 1, :] = jnp.where(count == j, this, 0.0)
            count = count + this
    for d in (2, -2, 1, -1):
        for cc in range(CORES):
            arrived(q_all.at[q_rows(mod(z - d, zn), x, cc)], qz_r.at[d % zn, cc])
        for hop in onward.get(d, ()):
            qz.append(along_z(pair_from(d), d, hop, d + hop, lambda n: qz_s.at[n, 0], lambda n: qz_r.at[n, 0]))
        along_x(d)

    for e, f in group:
        arrived(w_mine.at[mod(x - e, XN), mod(c - f, CORES)], wx_r.at[e, f])
    cols = out_ref.shape[0]
    every = [w_mine[xx, cc][:, 0:cols] for xx in range(XN) for cc in range(CORES)]
    w_wide[...] = jnp.concatenate(every, axis=1)
    wy = []

    def weights(src, origin, to, which):
        copy = remote(src, w_all.at[mod(origin + to + yn, yn)], wy_s.at[which], wy_r.at[which], dev(z, x, c, mod(to + yn, yn)))
        copy.start()
        wy.append(copy)

    for d in (2, -2, 1, -1):
        weights(w_wide, y, y + d, d % yn)
    w_all[mod(y + y, yn)] = w_wide[...]
    distant = (3, -3, 4)
    for d in distant:
        arrived(pair_from(d), qz_r.at[d % zn, 0])

    def tell(sem):
        for d in near:
            pl.semaphore_signal(sem, inc=1, device_id=dev(z, x, c, mod(y + d, yn)), device_id_type=MESH)

    tell(ready)

    def head_of(d, xx, h):
        return q_all.at[q_pair(mod(z - d, zn), xx), pl.ds(h * HD, HD)]

    for h in range(heads):
        for n, d in enumerate(distant):
            for e in near_first(XN):
                mine = head_of(d, x, h)
                copy = remote(mine, mine, qh_s.at[h, n, e], qh_r.at[h, n, e], dev(z, mod(x + e, XN), c, y))
                copy.start()
                qx.append(copy)
    v_own.wait()
    for h in range(heads):
        v_t[c, h * HD : (h + 1) * HD, :] = v_buf[c, :, h * HD : (h + 1) * HD].T
    k_own.wait()
    for copy in kv:
        copy.wait_recv()
    for h in range(heads):
        v_t[sib, h * HD : (h + 1) * HD, :] = v_buf[sib, :, h * HD : (h + 1) * HD].T
    for d in (0,) + near:
        for e in near_first(XN):
            arrived(q_all.at[q_pair(mod(z - d, zn), mod(x - e, XN))], qx_r.at[d % zn, e])

    scale = HD**-0.5 * math.log2(math.e)

    def choose(h):
        for n, d in enumerate(distant):
            for e in near_first(XN):
                arrived(head_of(d, mod(x - e, XN), h), qh_r.at[h, n, e])
        cols = slice(h * HD, (h + 1) * HD)

        def slot(i, _):
            rows = pl.ds(pl.multiple_of((i % MOST) * QB, QB), QB)
            picked = [masks[b, pl.ds(i, 1), :].astype(BF) * q_all[b * QB : (b + 1) * QB, cols] for b in range(nb)]
            q_sel[i // MOST, h, rows, :] = functools.reduce(jnp.add, picked)
            return 0

        lax.fori_loop(0, CORES * MOST, slot, 0)

    def front(h, cb):
        cols = slice(h * HD, (h + 1) * HD)
        s = lax.dot_general(k_buf[cb, :, cols], q_sel[cb, h], NT, preferred_element_type=F32)
        score[cb] = s
        peak[cb] = jnp.broadcast_to(jnp.max(s, axis=0, keepdims=True) * scale, (8, MOST * QB))

    def back(h, cb):
        cols = slice(h * HD, (h + 1) * HD)
        m = peak[cb, 0:1]
        e = jnp.exp2(score[cb] * scale - m)
        l = jnp.sum(e, axis=0, keepdims=True)
        o = jnp.dot(v_t[cb, cols, :], e.astype(BF), preferred_element_type=F32)
        for j in range(MOST):
            lanes = slice(j * QB, (j + 1) * QB)
            num[cb, j, cols, :] = o[:, lanes]
            top[cb, j, h : h + 1, :] = m[:, lanes]
            tot[cb, j, h : h + 1, :] = l[:, lanes]

    row = lax.broadcasted_iota(jnp.int32, (8, QB), 0)

    def stats_of(m, l):
        high = l.astype(BF).astype(F32)
        first = jnp.where(row < heads, m, pltpu.roll(high, heads, 0))
        return jnp.concatenate([first, l - high], axis=0).astype(BF)

    def read_stats(block):
        block = block.astype(F32)
        first = block[0:8]
        return first, pltpu.roll(first, 8 - heads, 0) + block[8:16]

    rx = []
    slots = range(CORES * MOST)

    def turn(i):
        return mod(z - y + i + 1 + yn, nb)

    def partial(h, b, xx):
        f = weight[b, h]
        rows = slice(h * HD + xx * dq, h * HD + (xx + 1) * dq)
        terms = [f[i : i + 1] * num[i // MOST, i % MOST, rows, :] for i in slots]
        return functools.reduce(jnp.add, terms).astype(BF)

    def weigh(h, b):
        mask = masks[b]
        tops = jnp.concatenate([top[i // MOST, i % MOST, h : h + 1, :] for i in slots], axis=0)
        tots = jnp.concatenate([tot[i // MOST, i % MOST, h : h + 1, :] for i in slots], axis=0)
        tops = jnp.where(mask > 0.5, tops, LOW)
        m = jnp.max(tops, axis=0, keepdims=True).astype(BF).astype(F32)
        f = jnp.exp2(tops - m)
        weight[b, h] = f
        stat_m[b, h : h + 1, :] = m
        stat_l[b, h : h + 1, :] = jnp.sum(f * tots, axis=0, keepdims=True)

    choose(0)
    front(0, 0)
    for h in range(heads):
        front(h, 1)
        back(h, 0)
        if h + 1 < heads:
            choose(h + 1)
            front(h + 1, 0)
        back(h, 1)
        if h + 1 < heads:

            def whole(b, _):
                weigh(h, b)
                for xx in range(XN):
                    parts[xx, h, b] = partial(h, b, xx)
                return 0

            lax.fori_loop(0, nb, whole, 0)
            for e in near_first(XN):
                to = mod(x + e, XN)
                copy = remote(parts.at[to, h], parts_in.at[e, h], rx_s.at[e, nb + h], rx_r.at[e, nb + h], dev(z, to, c, y))
                copy.start()
                rx.append(copy)
        if h == 0:
            pl.semaphore_wait(ready, len(near))
            tell(ready_all)
        if h == 1:
            for d, hops in far:
                origin = y + d
                arrived(w_all.at[mod(y + origin + yn, yn)], wy_r.at[-d % yn])
                for hop in hops:
                    weights(w_all.at[mod(origin + y + yn, yn)], origin, y + hop, (hop - d) % yn)

    for i in range(nb):
        b = turn(i)
        weigh(heads - 1, b)
        stats = stats_of(stat_m[b], stat_l[b])
        for xx in range(XN):
            ends[xx, b, 0:dq, :] = partial(heads - 1, b, xx)
            ends[xx, b, dq:, :] = stats
        for e in near_first(XN):
            to = mod(x + e, XN)
            copy = remote(ends.at[to, b], ends_in.at[e, b], rx_s.at[e, i], rx_r.at[e, i], dev(z, to, c, y))
            copy.start()
            rx.append(copy)

    def merge(all_stats, blocks):
        stats = [read_stats(block) for block in all_stats]
        m = functools.reduce(jnp.maximum, [s[0] for s in stats])
        factors = [jnp.exp2(s[0] - m) for s in stats]
        l = functools.reduce(jnp.add, [f * s[1] for f, s in zip(factors, stats)])
        sums_of = []
        for h in range(heads):
            terms = [f[h : h + 1] * block.astype(F32) for f, block in zip(factors, blocks[h])]
            sums_of.append(functools.reduce(jnp.add, terms))
        return sums_of, m, l

    pl.semaphore_wait(ready_all, len(near))
    for h in range(heads - 1):
        for e in near_first(XN):
            arrived(parts_in.at[e, h], rx_r.at[e, nb + h])
    for i in range(nb):
        b = turn(i)
        for e in near_first(XN):
            arrived(ends_in.at[e, b], rx_r.at[e, i])
        blocks = [[parts[x, h, b]] + [parts_in[e, h, b] for e in near_first(XN)] for h in range(heads - 1)]
        got = [ends[x, b]] + [ends_in[e, b] for e in near_first(XN)]
        blocks.append([block[0:dq] for block in got])
        merged, m, l = merge([block[dq:] for block in got], blocks)
        for h in range(heads):
            sums[i, h * dq : (h + 1) * dq, :] = merged[h].astype(BF)
        sums[i, body:, :] = stats_of(m, l)
        zz = mod(z + i + 1, zn)
        here = jnp.logical_and(zz == z, b == y)

        @pl.when(here)
        def _():
            pltpu.make_async_copy(sums.at[i], sums_in.at[z], rz_r.at[z]).start()

        @pl.when(jnp.logical_not(here))
        def _():
            remote(sums.at[i], sums_in.at[z], rz_s.at[i], rz_r.at[z], dev(zz, x, c, b)).start()

    for zz in range(zn):
        arrived(sums_in.at[zz], rz_r.at[zz])
    got = [sums_in[zz] for zz in range(zn)]
    blocks = [[block[h * dq : (h + 1) * dq] for block in got] for h in range(heads)]
    merged, m, l = merge([block[body:] for block in got], blocks)
    for h in range(heads):
        att[z, h * dq : (h + 1) * dq, :] = (merged[h] / l[h : h + 1]).astype(BF)

    def rz_wait():
        for i in range(nb):
            b = turn(i)
            here = jnp.logical_and(mod(z + i + 1, zn) == z, b == y)

            @pl.when(jnp.logical_not(here))
            def _():
                remote(sums.at[i], sums_in.at[z], rz_s.at[i], rz_r.at[z], dev(z, x, c, y)).wait_send()

    az = [along_z(att.at[z], 0, d, d, lambda n: az_s.at[n], lambda n: az_r.at[n]) for d in near]
    for d in (2, -2):
        piece = att.at[mod(z - d, zn)]
        arrived(piece, az_r.at[d % zn])
        for hop in onward[d]:
            az.append(along_z(piece, d, hop, d + hop, lambda n: az_s.at[n], lambda n: az_r.at[n]))
    for d in range(1, yn):
        if d not in (2, yn - 2):
            arrived(w_all.at[mod(y + y - d + yn, yn)], wy_r.at[d])
    w_turned[...] = w_all[...].reshape(zn * body, w_all.shape[2]).T
    for d in (1, -1, 3, -3, 4):
        arrived(att.at[mod(z - d, zn)], az_r.at[d % zn])

    rows = att[...].reshape(zn * body, QB)
    outs = []
    for e, f in group + [(0, 0)]:
        xx, cc = mod(x + e, XN), mod(c + f, CORES)
        wide = w_turned[pl.ds(pl.multiple_of((xx * CORES + cc) * cols, cols), cols), :]
        term = jnp.dot(wide, rows, preferred_element_type=F32)
        if e or f:
            out_part[xx, cc] = term.astype(BF)
            copy = remote(out_part.at[xx, cc], out_in.at[e, f], out_s.at[e, f], out_r.at[e, f], dev(z, xx, cc, y))
            copy.start()
            outs.append(copy)
    for sent in (qz, qx, kv, wx, wy, rx, az):
        for copy in sent:
            copy.wait_send()
    rz_wait()
    for copy in outs:
        copy.wait()
    for e, f in group:
        term = term + out_in[e, f].astype(F32)
    out_ref[...] = term.astype(BF)


def shards(queries, keys, values, pattern, out_weight):
    yn = lax.axis_size("heads")
    zn = lax.axis_size("rows") // (XN * CORES)
    nb = pattern.shape[0]
    own, width = queries.shape
    half = width // CORES
    heads = half // HD
    cblk = keys.shape[0]
    cols = out_weight.shape[1]
    piece = heads * (HD // XN)
    load = piece + STATS
    dma = pltpu.SemaphoreType.DMA
    anywhere = pl.BlockSpec(memory_space=pl.ANY)
    return pl.pallas_call(
        kernel,
        name="attend_project",
        out_shape=jax.ShapeDtypeStruct((cols, QB), BF),
        in_specs=[anywhere, anywhere, anywhere, pl.BlockSpec(memory_space=pltpu.VMEM), anywhere],
        out_specs=pl.BlockSpec(memory_space=pltpu.VMEM),
        scratch_shapes=[
            pltpu.VMEM((nb * QB, half), BF),
            pltpu.VMEM((CORES, cblk, half), BF),
            pltpu.VMEM((CORES, cblk, half), BF),
            pltpu.VMEM((CORES, half, cblk), BF),
            pltpu.VMEM((LANES, width), BF),
            pltpu.VMEM((XN, CORES, piece, LANES), BF),
            pltpu.VMEM((XN, CORES, piece, LANES), BF),
            pltpu.VMEM((piece, XN * CORES * cols), BF),
            pltpu.VMEM((yn, piece, XN * CORES * cols), BF),
            pltpu.VMEM((XN * CORES * cols, zn * piece), BF),
            pltpu.VMEM((CORES, heads, MOST * QB, HD), BF),
            pltpu.VMEM((2, cblk, MOST * QB), F32),
            pltpu.VMEM((2, 8, MOST * QB), F32),
            pltpu.VMEM((CORES, MOST, half, QB), F32),
            pltpu.VMEM((CORES, MOST, 8, QB), F32),
            pltpu.VMEM((CORES, MOST, 8, QB), F32),
            pltpu.VMEM((XN, heads - 1, nb, HD // XN, QB), BF),
            pltpu.VMEM((XN, heads - 1, nb, HD // XN, QB), BF),
            pltpu.VMEM((XN, nb, HD // XN + STATS, QB), BF),
            pltpu.VMEM((XN, nb, HD // XN + STATS, QB), BF),
            pltpu.VMEM((nb, heads, CORES * MOST, QB), F32),
            pltpu.VMEM((nb, 8, QB), F32),
            pltpu.VMEM((nb, 8, QB), F32),
            pltpu.VMEM((nb, load, QB), BF),
            pltpu.VMEM((zn, load, QB), BF),
            pltpu.VMEM((zn, piece, QB), BF),
            pltpu.VMEM((XN, CORES, cols, QB), BF),
            pltpu.VMEM((XN, CORES, cols, QB), BF),
            pltpu.VMEM((nb, CORES * MOST, QB), F32),
            dma((4,)),
            dma((zn, CORES)),
            dma((zn, CORES)),
            dma((zn, XN)),
            dma((zn, XN)),
            dma((2,)),
            dma((2,)),
            dma((XN, CORES)),
            dma((XN, CORES)),
            dma((yn,)),
            dma((yn,)),
            dma((heads, 3, XN)),
            dma((heads, 3, XN)),
            dma((XN, nb + heads - 1)),
            dma((XN, nb + heads - 1)),
            dma((nb,)),
            dma((zn,)),
            dma((zn,)),
            dma((zn,)),
            dma((XN, CORES)),
            dma((XN, CORES)),
            pltpu.SemaphoreType.REGULAR,
            pltpu.SemaphoreType.REGULAR,
        ],
        compiler_params=pltpu.CompilerParams(
            collective_id=0, has_side_effects=True, vmem_limit_bytes=64 * 2**20
        ),
        cost_estimate=pl.CostEstimate(flops=3 * 10**9, bytes_accessed=4 * 10**6, transcendentals=3 * 10**6),
    )(queries, keys, values, pattern, out_weight.T).T


def solution(mesh):
    in_specs = (P("rows", "heads"), P("rows", "heads"), P("rows", "heads"), P(), P("heads", "rows"))
    out_specs = P("heads", "rows")
    return jax.shard_map(shards, mesh=mesh, in_specs=in_specs, out_specs=out_specs, check_vma=False)
```

```python
import functools
import math

import jax
import jax.numpy as jnp
from jax import lax
from jax.experimental import pallas as pl
from jax.experimental.pallas import tpu as pltpu
from jax.sharding import PartitionSpec as P

MESH = pl.DeviceIdType.MESH
HD = 128
QB = 128
MOST = 4
CORES = 2
XN = 4
STATS = 16
LANES = 128
LOW = -(2.0**100)
NT = (((1,), (1,)), ((), ()))
BF = jnp.bfloat16
F32 = jnp.float32


def near_first(n):
    order = []
    for step in range(1, n // 2 + 1):
        order.append(step)
        if n - step != step:
            order.append(n - step)
    return order


def kernel(
    q_ref,
    k_ref,
    v_ref,
    pat_ref,
    w_ref,
    out_ref,
    q_all,
    k_buf,
    v_buf,
    v_t,
    w_in,
    w_piece,
    w_mine,
    w_wide,
    w_all,
    w_turned,
    q_sel,
    score,
    peak,
    num,
    top,
    tot,
    parts,
    parts_in,
    ends,
    ends_in,
    weight,
    stat_m,
    stat_l,
    sums,
    sums_in,
    att,
    out_part,
    out_in,
    masks,
    local_sem,
    qz_s,
    qz_r,
    qx_s,
    qx_r,
    kv_s,
    kv_r,
    wx_s,
    wx_r,
    wy_s,
    wy_r,
    qh_s,
    qh_r,
    rx_s,
    rx_r,
    rz_s,
    rz_r,
    az_s,
    az_r,
    out_s,
    out_r,
    ready,
    ready_all,
):
    r = lax.axis_index("rows")
    y = lax.axis_index("heads")
    yn = w_all.shape[0]
    zn = att.shape[0]
    nb = zn
    heads = num.shape[2] // HD
    half = heads * HD
    dq = HD // XN
    body = heads * dq
    own = q_ref.shape[0]
    z = r // (XN * CORES)
    x = (r // CORES) % XN
    c = r % CORES
    sib = 1 - c

    def dev(dz, dx, dc, dy):
        return ((dz * XN + dx) * CORES + dc, dy)

    def remote(src, dst, ss, rs, to):
        return pltpu.make_async_remote_copy(
            src_ref=src, dst_ref=dst, send_sem=ss, recv_sem=rs, device_id=to, device_id_type=MESH
        )

    def mod(v, n):
        return lax.rem(v + n, n)

    def half_of(which):
        return pl.ds(pl.multiple_of(which * half, HD), half)

    def q_rows(zz, xx, cc):
        return pl.ds(pl.multiple_of((zz * XN + xx) * (CORES * own) + cc * own, own), own)

    def q_pair(zz, xx):
        return pl.ds(pl.multiple_of((zz * XN + xx) * (CORES * own), CORES * own), CORES * own)

    k_own = pltpu.make_async_copy(k_ref.at[:, half_of(c)], k_buf.at[c], local_sem.at[0])
    v_own = pltpu.make_async_copy(v_ref.at[:, half_of(c)], v_buf.at[c], local_sem.at[1])
    q_own = pltpu.make_async_copy(q_ref.at[:, half_of(c)], q_all.at[q_rows(z, x, c)], local_sem.at[2])
    w_own = pltpu.make_async_copy(w_ref, w_in.at[0 : w_ref.shape[0]], local_sem.at[3])
    q_own.start()
    w_own.start()
    v_own.start()
    k_own.start()

    bar = pltpu.get_barrier_semaphore()

    def signal(to):
        pl.semaphore_signal(bar, inc=1, device_id=to, device_id_type=MESH)

    near = (1, -1, 2, -2)
    far = ((2, (-1, -2)), (-2, (1,)))
    onward = {2: (1, 2), -2: (-1,)}
    group = [(e, f) for e in (2, 1, 3, 0) for f in (1, 0) if e or f]
    for d in reversed(near):
        for cc in range(CORES):
            signal(dev(mod(z + d, zn), x, cc, y))
        signal(dev(z, x, c, mod(y + d, yn)))
    for e, f in group:
        signal(dev(z, mod(x + e, XN), mod(c + f, CORES), y))
    signals = len(near) * (CORES + 1) + len(group)

    pl.semaphore_wait(bar, signals)

    rows_here = q_all.at[q_rows(z, x, c)]
    qz, qx = [], []

    def half_to(cc, d, ss):
        copy = remote(q_ref.at[:, half_of(cc)], rows_here, ss, qz_r.at[d % zn, c], dev(mod(z + d, zn), x, cc, y))
        copy.start()
        qz.append(copy)

    half_to(sib, 0, qz_s.at[0, 0])
    for d in near:
        for cc in range(CORES):
            half_to(cc, d, qz_s.at[d % zn, cc])

    def arrived(dst, sem):
        pltpu.make_async_copy(dst, dst, sem).wait()

    def along_z(ref, origin, hop, distance, ss, rs):
        copy = remote(ref, ref, ss(distance % zn), rs(distance % zn), dev(mod(z + hop, zn), x, c, y))
        copy.start()
        return copy

    def pair_from(d):
        return q_all.at[q_pair(mod(z - d, zn), x)]


    def along_x(d):
        for e in near_first(XN):
            pair = pair_from(d)
            copy = remote(pair, pair, qx_s.at[d % zn, e], qx_r.at[d % zn, e], dev(z, mod(x + e, XN), c, y))
            copy.start()
            qx.append(copy)

    q_own.wait()
    arrived(q_all.at[q_rows(z, x, sib)], qz_r.at[0, sib])
    along_x(0)
    kv = [
        remote(ref.at[:, half_of(sib)], buf.at[c], kv_s.at[i], kv_r.at[i], dev(z, x, sib, y))
        for i, (ref, buf) in enumerate(((k_ref, k_buf), (v_ref, v_buf)))
    ]
    for copy in kv:
        copy.start()

    w_in[w_ref.shape[0] :, :] = jnp.zeros((LANES - w_ref.shape[0], w_in.shape[1]), BF)
    w_own.wait()
    for cc in range(CORES):
        for h in range(heads):
            first = cc * half + h * HD
            turned = w_in[:, first : first + HD].astype(F32).T.astype(BF)
            for xx in range(XN):
                w_piece[xx, cc, h * dq : (h + 1) * dq, :] = turned[xx * dq : (xx + 1) * dq]
    w_mine[x, c] = w_piece[x, c]
    wx = []
    for e, f in group:
        to = mod(x + e, XN), mod(c + f, CORES)
        copy = remote(w_piece.at[to[0], to[1]], w_mine.at[x, c], wx_s.at[e, f], wx_r.at[e, f], dev(z, to[0], to[1], y))
        copy.start()
        wx.append(copy)

    top[...] = jnp.zeros_like(top)
    tot[...] = jnp.zeros_like(tot)
    stat_m[...] = jnp.zeros_like(stat_m)
    stat_l[...] = jnp.zeros_like(stat_l)

    for cb in range(CORES):
        hit = (pat_ref[...] == (z * XN + x) * CORES + cb).astype(F32)
        linked = jnp.max(hit, axis=1, keepdims=True)
        count = jnp.zeros((1, QB), F32)
        for b in range(nb):
            this = jnp.broadcast_to(linked[b : b + 1], (1, QB))
            for j in range(MOST):
                masks[b, cb * MOST + j : cb * MOST + j + 1, :] = jnp.where(count == j, this, 0.0)
            count = count + this
    for d in (2, -2, 1, -1):
        for cc in range(CORES):
            arrived(q_all.at[q_rows(mod(z - d, zn), x, cc)], qz_r.at[d % zn, cc])
        for hop in onward.get(d, ()):
            qz.append(along_z(pair_from(d), d, hop, d + hop, lambda n: qz_s.at[n, 0], lambda n: qz_r.at[n, 0]))
        along_x(d)

    for e, f in group:
        arrived(w_mine.at[mod(x - e, XN), mod(c - f, CORES)], wx_r.at[e, f])
    cols = out_ref.shape[0]
    every = [w_mine[xx, cc][:, 0:cols] for xx in range(XN) for cc in range(CORES)]
    w_wide[...] = jnp.concatenate(every, axis=1)
    wy = []

    def weights(src, origin, to, which):
        copy = remote(src, w_all.at[mod(origin + to + yn, yn)], wy_s.at[which], wy_r.at[which], dev(z, x, c, mod(to + yn, yn)))
        copy.start()
        wy.append(copy)

    for d in (2, -2, 1, -1):
        weights(w_wide, y, y + d, d % yn)
    w_all[mod(y + y, yn)] = w_wide[...]
    distant = (3, -3, 4)
    for d in distant:
        arrived(pair_from(d), qz_r.at[d % zn, 0])

    def tell(sem):
        for d in near:
            pl.semaphore_signal(sem, inc=1, device_id=dev(z, x, c, mod(y + d, yn)), device_id_type=MESH)

    tell(ready)

    def head_of(d, xx, h):
        return q_all.at[q_pair(mod(z - d, zn), xx), pl.ds(h * HD, HD)]

    for h in range(heads):
        for n, d in enumerate(distant):
            for e in near_first(XN):
                mine = head_of(d, x, h)
                copy = remote(mine, mine, qh_s.at[h, n, e], qh_r.at[h, n, e], dev(z, mod(x + e, XN), c, y))
                copy.start()
                qx.append(copy)
    v_own.wait()
    for h in range(heads):
        v_t[c, h * HD : (h + 1) * HD, :] = v_buf[c, :, h * HD : (h + 1) * HD].T
    k_own.wait()
    for copy in kv:
        copy.wait_recv()
    for h in range(heads):
        v_t[sib, h * HD : (h + 1) * HD, :] = v_buf[sib, :, h * HD : (h + 1) * HD].T
    for d in (0,) + near:
        for e in near_first(XN):
            arrived(q_all.at[q_pair(mod(z - d, zn), mod(x - e, XN))], qx_r.at[d % zn, e])

    scale = HD**-0.5 * math.log2(math.e)

    def choose(h):
        for n, d in enumerate(distant):
            for e in near_first(XN):
                arrived(head_of(d, mod(x - e, XN), h), qh_r.at[h, n, e])
        cols = slice(h * HD, (h + 1) * HD)

        def slot(i, _):
            rows = pl.ds(pl.multiple_of((i % MOST) * QB, QB), QB)
            picked = [masks[b, pl.ds(i, 1), :].astype(BF) * q_all[b * QB : (b + 1) * QB, cols] for b in range(nb)]
            q_sel[i // MOST, h, rows, :] = functools.reduce(jnp.add, picked)
            return 0

        lax.fori_loop(0, CORES * MOST, slot, 0)

    def front(h, cb):
        cols = slice(h * HD, (h + 1) * HD)
        s = lax.dot_general(k_buf[cb, :, cols], q_sel[cb, h], NT, preferred_element_type=F32)
        score[cb] = s
        peak[cb] = jnp.broadcast_to(jnp.max(s, axis=0, keepdims=True) * scale, (8, MOST * QB))

    def back(h, cb):
        cols = slice(h * HD, (h + 1) * HD)
        m = peak[cb, 0:1]
        e = jnp.exp2(score[cb] * scale - m)
        l = jnp.sum(e, axis=0, keepdims=True)
        o = jnp.dot(v_t[cb, cols, :], e.astype(BF), preferred_element_type=F32)
        for j in range(MOST):
            lanes = slice(j * QB, (j + 1) * QB)
            num[cb, j, cols, :] = o[:, lanes]
            top[cb, j, h : h + 1, :] = m[:, lanes]
            tot[cb, j, h : h + 1, :] = l[:, lanes]

    row = lax.broadcasted_iota(jnp.int32, (8, QB), 0)

    def stats_of(m, l):
        high = l.astype(BF).astype(F32)
        first = jnp.where(row < heads, m, pltpu.roll(high, heads, 0))
        return jnp.concatenate([first, l - high], axis=0).astype(BF)

    def read_stats(block):
        block = block.astype(F32)
        first = block[0:8]
        return first, pltpu.roll(first, 8 - heads, 0) + block[8:16]

    rx = []
    slots = range(CORES * MOST)

    def turn(i):
        return mod(z - y + i + 1 + yn, nb)

    def partial(h, b, xx):
        f = weight[b, h]
        rows = slice(h * HD + xx * dq, h * HD + (xx + 1) * dq)
        terms = [f[i : i + 1] * num[i // MOST, i % MOST, rows, :] for i in slots]
        return functools.reduce(jnp.add, terms).astype(BF)

    def weigh(h, b):
        mask = masks[b]
        tops = jnp.concatenate([top[i // MOST, i % MOST, h : h + 1, :] for i in slots], axis=0)
        tots = jnp.concatenate([tot[i // MOST, i % MOST, h : h + 1, :] for i in slots], axis=0)
        tops = jnp.where(mask > 0.5, tops, LOW)
        m = jnp.max(tops, axis=0, keepdims=True).astype(BF).astype(F32)
        f = jnp.exp2(tops - m)
        weight[b, h] = f
        stat_m[b, h : h + 1, :] = m
        stat_l[b, h : h + 1, :] = jnp.sum(f * tots, axis=0, keepdims=True)

    choose(0)
    front(0, 0)
    for h in range(heads):
        front(h, 1)
        back(h, 0)
        if h + 1 < heads:
            choose(h + 1)
            front(h + 1, 0)
        back(h, 1)
        if h + 1 < heads:

            def whole(b, _):
                weigh(h, b)
                for xx in range(XN):
                    parts[xx, h, b] = partial(h, b, xx)
                return 0

            lax.fori_loop(0, nb, whole, 0)
            for e in near_first(XN):
                to = mod(x + e, XN)
                copy = remote(parts.at[to, h], parts_in.at[e, h], rx_s.at[e, nb + h], rx_r.at[e, nb + h], dev(z, to, c, y))
                copy.start()
                rx.append(copy)
        if h == 0:
            pl.semaphore_wait(ready, len(near))
            tell(ready_all)
    for i in range(nb):
        b = turn(i)
        weigh(heads - 1, b)
        stats = stats_of(stat_m[b], stat_l[b])
        for xx in range(XN):
            ends[xx, b, 0:dq, :] = partial(heads - 1, b, xx)
            ends[xx, b, dq:, :] = stats
        for e in near_first(XN):
            to = mod(x + e, XN)
            copy = remote(ends.at[to, b], ends_in.at[e, b], rx_s.at[e, i], rx_r.at[e, i], dev(z, to, c, y))
            copy.start()
            rx.append(copy)

    for d, hops in far:
        origin = y + d
        arrived(w_all.at[mod(y + origin + yn, yn)], wy_r.at[-d % yn])
        for hop in hops:
            weights(w_all.at[mod(origin + y + yn, yn)], origin, y + hop, (hop - d) % yn)

    def merge(all_stats, blocks):
        stats = [read_stats(block) for block in all_stats]
        m = functools.reduce(jnp.maximum, [s[0] for s in stats])
        factors = [jnp.exp2(s[0] - m) for s in stats]
        l = functools.reduce(jnp.add, [f * s[1] for f, s in zip(factors, stats)])
        sums_of = []
        for h in range(heads):
            terms = [f[h : h + 1] * block.astype(F32) for f, block in zip(factors, blocks[h])]
            sums_of.append(functools.reduce(jnp.add, terms))
        return sums_of, m, l

    pl.semaphore_wait(ready_all, len(near))
    for h in range(heads - 1):
        for e in near_first(XN):
            arrived(parts_in.at[e, h], rx_r.at[e, nb + h])
    for i in range(nb):
        b = turn(i)
        for e in near_first(XN):
            arrived(ends_in.at[e, b], rx_r.at[e, i])
        blocks = [[parts[x, h, b]] + [parts_in[e, h, b] for e in near_first(XN)] for h in range(heads - 1)]
        got = [ends[x, b]] + [ends_in[e, b] for e in near_first(XN)]
        blocks.append([block[0:dq] for block in got])
        merged, m, l = merge([block[dq:] for block in got], blocks)
        for h in range(heads):
            sums[i, h * dq : (h + 1) * dq, :] = merged[h].astype(BF)
        sums[i, body:, :] = stats_of(m, l)
        zz = mod(z + i + 1, zn)
        here = jnp.logical_and(zz == z, b == y)

        @pl.when(here)
        def _():
            pltpu.make_async_copy(sums.at[i], sums_in.at[z], rz_r.at[z]).start()

        @pl.when(jnp.logical_not(here))
        def _():
            remote(sums.at[i], sums_in.at[z], rz_s.at[i], rz_r.at[z], dev(zz, x, c, b)).start()

    for zz in range(zn):
        arrived(sums_in.at[zz], rz_r.at[zz])
    got = [sums_in[zz] for zz in range(zn)]
    blocks = [[block[h * dq : (h + 1) * dq] for block in got] for h in range(heads)]
    merged, m, l = merge([block[body:] for block in got], blocks)
    for h in range(heads):
        att[z, h * dq : (h + 1) * dq, :] = (merged[h] / l[h : h + 1]).astype(BF)

    def rz_wait():
        for i in range(nb):
            b = turn(i)
            here = jnp.logical_and(mod(z + i + 1, zn) == z, b == y)

            @pl.when(jnp.logical_not(here))
            def _():
                remote(sums.at[i], sums_in.at[z], rz_s.at[i], rz_r.at[z], dev(z, x, c, y)).wait_send()

    az = [along_z(att.at[z], 0, d, d, lambda n: az_s.at[n], lambda n: az_r.at[n]) for d in near]
    for d in (2, -2):
        piece = att.at[mod(z - d, zn)]
        arrived(piece, az_r.at[d % zn])
        for hop in onward[d]:
            az.append(along_z(piece, d, hop, d + hop, lambda n: az_s.at[n], lambda n: az_r.at[n]))
    for d in range(1, yn):
        if d not in (2, yn - 2):
            arrived(w_all.at[mod(y + y - d + yn, yn)], wy_r.at[d])
    w_turned[...] = w_all[...].reshape(zn * body, w_all.shape[2]).T
    for d in (1, -1, 3, -3, 4):
        arrived(att.at[mod(z - d, zn)], az_r.at[d % zn])

    rows = att[...].reshape(zn * body, QB)
    outs = []
    for e, f in group + [(0, 0)]:
        xx, cc = mod(x + e, XN), mod(c + f, CORES)
        wide = w_turned[pl.ds(pl.multiple_of((xx * CORES + cc) * cols, cols), cols), :]
        term = jnp.dot(wide, rows, preferred_element_type=F32)
        if e or f:
            out_part[xx, cc] = term.astype(BF)
            copy = remote(out_part.at[xx, cc], out_in.at[e, f], out_s.at[e, f], out_r.at[e, f], dev(z, xx, cc, y))
            copy.start()
            outs.append(copy)
    for sent in (qz, qx, kv, wx, wy, rx, az):
        for copy in sent:
            copy.wait_send()
    rz_wait()
    for copy in outs:
        copy.wait()
    for e, f in group:
        term = term + out_in[e, f].astype(F32)
    out_ref[...] = term.astype(BF)


def shards(queries, keys, values, pattern, out_weight):
    yn = lax.axis_size("heads")
    zn = lax.axis_size("rows") // (XN * CORES)
    nb = pattern.shape[0]
    own, width = queries.shape
    half = width // CORES
    heads = half // HD
    cblk = keys.shape[0]
    cols = out_weight.shape[1]
    piece = heads * (HD // XN)
    load = piece + STATS
    dma = pltpu.SemaphoreType.DMA
    anywhere = pl.BlockSpec(memory_space=pl.ANY)
    return pl.pallas_call(
        kernel,
        name="attend_project",
        out_shape=jax.ShapeDtypeStruct((cols, QB), BF),
        in_specs=[anywhere, anywhere, anywhere, pl.BlockSpec(memory_space=pltpu.VMEM), anywhere],
        out_specs=pl.BlockSpec(memory_space=pltpu.VMEM),
        scratch_shapes=[
            pltpu.VMEM((nb * QB, half), BF),
            pltpu.VMEM((CORES, cblk, half), BF),
            pltpu.VMEM((CORES, cblk, half), BF),
            pltpu.VMEM((CORES, half, cblk), BF),
            pltpu.VMEM((LANES, width), BF),
            pltpu.VMEM((XN, CORES, piece, LANES), BF),
            pltpu.VMEM((XN, CORES, piece, LANES), BF),
            pltpu.VMEM((piece, XN * CORES * cols), BF),
            pltpu.VMEM((yn, piece, XN * CORES * cols), BF),
            pltpu.VMEM((XN * CORES * cols, zn * piece), BF),
            pltpu.VMEM((CORES, heads, MOST * QB, HD), BF),
            pltpu.VMEM((2, cblk, MOST * QB), F32),
            pltpu.VMEM((2, 8, MOST * QB), F32),
            pltpu.VMEM((CORES, MOST, half, QB), F32),
            pltpu.VMEM((CORES, MOST, 8, QB), F32),
            pltpu.VMEM((CORES, MOST, 8, QB), F32),
            pltpu.VMEM((XN, heads - 1, nb, HD // XN, QB), BF),
            pltpu.VMEM((XN, heads - 1, nb, HD // XN, QB), BF),
            pltpu.VMEM((XN, nb, HD // XN + STATS, QB), BF),
            pltpu.VMEM((XN, nb, HD // XN + STATS, QB), BF),
            pltpu.VMEM((nb, heads, CORES * MOST, QB), F32),
            pltpu.VMEM((nb, 8, QB), F32),
            pltpu.VMEM((nb, 8, QB), F32),
            pltpu.VMEM((nb, load, QB), BF),
            pltpu.VMEM((zn, load, QB), BF),
            pltpu.VMEM((zn, piece, QB), BF),
            pltpu.VMEM((XN, CORES, cols, QB), BF),
            pltpu.VMEM((XN, CORES, cols, QB), BF),
            pltpu.VMEM((nb, CORES * MOST, QB), F32),
            dma((4,)),
            dma((zn, CORES)),
            dma((zn, CORES)),
            dma((zn, XN)),
            dma((zn, XN)),
            dma((2,)),
            dma((2,)),
            dma((XN, CORES)),
            dma((XN, CORES)),
            dma((yn,)),
            dma((yn,)),
            dma((heads, 3, XN)),
            dma((heads, 3, XN)),
            dma((XN, nb + heads - 1)),
            dma((XN, nb + heads - 1)),
            dma((nb,)),
            dma((zn,)),
            dma((zn,)),
            dma((zn,)),
            dma((XN, CORES)),
            dma((XN, CORES)),
            pltpu.SemaphoreType.REGULAR,
            pltpu.SemaphoreType.REGULAR,
        ],
        compiler_params=pltpu.CompilerParams(
            collective_id=0, has_side_effects=True, vmem_limit_bytes=64 * 2**20
        ),
        cost_estimate=pl.CostEstimate(flops=3 * 10**9, bytes_accessed=4 * 10**6, transcendentals=3 * 10**6),
    )(queries, keys, values, pattern, out_weight.T).T


def solution(mesh):
    in_specs = (P("rows", "heads"), P("rows", "heads"), P("rows", "heads"), P(), P("heads", "rows"))
    out_specs = P("heads", "rows")
    return jax.shard_map(shards, mesh=mesh, in_specs=in_specs, out_specs=out_specs, check_vma=False)
```
